32 devices in a mesh: groups: 2 (over x), lat: 16 (over z, y, core).
Axes of the slice: x: 2, y: 2, z: 4, core: 2. Of those that a mesh axis runs over, the one named last changes fastest.
Arguments:
- grid: bfloat16 [1024, 16, 8192], P('lat', 'groups'), parts along dimension 1, may hold values from -6 to 6
- cycle_weights: float32 [1024], P('lat'), may hold values from 0.1 to 1
- order_ids: int32 [38], replicated, may hold values from 0 to 4095, as said below
- leaf_weight: bfloat16 [1024, 38, 64], P('lat'), may hold values from -0.75 to 0.75
- transfer: bfloat16 [4, 16, 38, 64, 128], P(None, 'lat'), may hold values from -0.5 to 0.5
- degree_weight: bfloat16 [4096, 38, 64], P('lat'), may hold values from -0.75 to 0.75
Outputs:
- spectrum: float32 [4096, 38, 32], P('lat', None, 'groups'), parts along dimension 2
The draws below stay inside these ranges and needn't reach their ends.
There are 2 independent parts, one for each index of `groups`. The reference program is written for one: setup_inputs(seed, part) draws one part's arguments, and reference() takes and returns one part's arrays. A program takes and returns all parts, laid end to end along the dimension named above; an argument that names none is the same for every part. Nothing has to cross between parts.
Inputs may be any that keep to these rules, and one draw needn't show every extreme that they name: `order_ids`: the 38 entries are distinct orders.
All inputs are finite; a program needn't handle non-finite values.
Results may differ from the reference program's by a relative error of at most 0.0023.
Values may be sent and summed in bfloat16 or wider, within the bound.
A program may use at most 64 MiB of HBM per device.

```python
import math
import jax
import jax.numpy as jnp
from jax import lax

FIELDS = 8
CYCLE_DEV = 64
NLON = 8192
DEGREES = 4096
ORDERS = 38
RANK = 64
CYCLES = 1024
LEVELS = 4
N_LAT = 16


def draw_order_ids(key, part):
    chosen = jax.random.permutation(key, DEGREES)[:ORDERS]
    return chosen.astype(jnp.int32)


def level_of(key, extent, pieces, smallest, largest):
    loudness, own = 1.0, jax.random.fold_in(key, 6)
    for dim, parts in pieces:
        steps = jnp.exp(jax.random.uniform(jax.random.fold_in(own, dim), (parts,), jnp.float32, smallest / len(pieces), largest / len(pieces)))
        loudness = loudness * jnp.repeat(steps, extent[dim] // parts).reshape([-1 if axis == dim else 1 for axis in range(len(extent))])
    return loudness


def scatter_about(key, extent, spread, most, cuts=(), dtype=jnp.bfloat16):
    factor_of = level_of(key, extent, cuts, -0.22, 0.18) if cuts else 1.0
    entries = jax.random.normal(key, extent, jnp.float32) * spread * factor_of
    return jnp.minimum(jnp.maximum(entries, -most), most).astype(dtype)


def setup_inputs(seed: int = 0, part: int = 0) -> dict:
    streams_of = jax.random.split(jax.random.key(seed), 7)
    part_splits = jax.random.split(jax.random.fold_in(streams_of[6], part), 7)
    return {
        "grid": scatter_about(part_splits[0], (CYCLES, FIELDS, NLON), 1.0, 6.0, ((0, 16),)),
        "cycle_weights": jnp.clip(jnp.exp(math.log(1.0) - 2.3025851 * jax.random.uniform(streams_of[1], (CYCLES,), jnp.float32) ** level_of(streams_of[1], (CYCLES,), ((0, 16),), -0.2, 0.2)), 0.1, 1.0),
        "order_ids": draw_order_ids(jax.random.fold_in(streams_of[6], 71), part),
        "leaf_weight": scatter_about(streams_of[3], (CYCLES, ORDERS, RANK), CYCLE_DEV ** -0.5, 0.75, ((0, 16),)),
        "transfer": scatter_about(streams_of[4], (LEVELS, N_LAT, ORDERS, RANK, 2 * RANK), (2 * RANK) ** -0.5, 0.5, ((1, 16),)),
        "degree_weight": scatter_about(streams_of[5], (DEGREES, ORDERS, RANK), RANK ** -0.5, 0.75, ((0, 16),)),
    }


def spectra(grid, cycle_weights, order_ids):
    cycles, fields, nlon = grid.shape
    count = order_ids.shape[0]
    longitude = lax.iota(jnp.int32, nlon)
    index = order_ids[:, None].astype(jnp.int32) * longitude[None, :] % nlon
    angle = index.astype(jnp.float32) * jnp.float32(2.0 * math.pi / nlon)
    table = jnp.concatenate([jnp.cos(angle), -jnp.sin(angle)], 0).astype(jnp.bfloat16)
    raw = jnp.dot(grid.reshape(cycles * fields, nlon), table.T, preferred_element_type=jnp.float32)
    raw = raw.reshape(cycles, fields, 2, count).transpose(0, 2, 1, 3).reshape(cycles, 2 * fields, count)
    return raw * (cycle_weights[:, None, None] / jnp.float32(math.sqrt(nlon)))

def reference(grid, cycle_weights, order_ids, leaf_weight, transfer, degree_weight):
    waves = spectra(grid, cycle_weights, order_ids)
    nodes = N_LAT
    width = waves.shape[1]
    blocks = waves.reshape(nodes, CYCLE_DEV, width, ORDERS)
    leaves = leaf_weight.astype(jnp.float32).reshape(nodes, CYCLE_DEV, ORDERS, RANK)
    current = jnp.einsum('nkor,nkqo->norq', leaves, blocks, precision=lax.Precision.HIGHEST)
    for level in range(LEVELS):
        span = 2 ** level
        groups = nodes // (2 * span)
        split = current.reshape(groups, 2, span, ORDERS, RANK, width)
        joined = jnp.concatenate([split[:, 0], split[:, 1]], axis=3)
        factors = transfer[level].astype(jnp.float32).reshape(groups, 2, span, ORDERS, RANK, 2 * RANK)
        current = jnp.einsum('gtpors,gposq->gtporq', factors, joined, precision=lax.Precision.HIGHEST)
        current = current.reshape(nodes, ORDERS, RANK, width)
    per_node = DEGREES // nodes
    finals = degree_weight.astype(jnp.float32).reshape(nodes, per_node, ORDERS, RANK)
    result = jnp.einsum('ndor,norq->ndoq', finals, current, precision=lax.Precision.HIGHEST)
    result = result.reshape(DEGREES, ORDERS, width)
    degree = lax.iota(jnp.int32, DEGREES)
    keep = degree[:, None] >= order_ids[None, :].astype(jnp.int32)
    return jnp.where(keep[:, :, None], result, jnp.float32(0.0))
```

```python
import functools
import math

import jax
import jax.numpy as jnp
from jax import lax
from jax.experimental import pallas as pl
from jax.experimental.pallas import tpu as pltpu
from jax.sharding import PartitionSpec as P

LANES = 128
NARROW_LEVELS = 3
MESH = pl.DeviceIdType.MESH


def split(x):
    high = x.astype(jnp.bfloat16)
    low = (x - high.astype(jnp.float32)).astype(jnp.bfloat16)
    return high, low


def kernel(
    dims,
    ids_ref,
    weight_ref,
    grid_hbm,
    leaf_hbm,
    transfer_hbm,
    degree_hbm,
    out_ref,
    grid_ref,
    leaf_ref,
    transfer_ref,
    degree_ref,
    table_ref,
    raw_ref,
    waves_ref,
    high_ref,
    low_ref,
    grid_sem,
    weight_sem,
    send_sem,
    recv_sem,
):
    orders, padded, rank, fields, cycles, nlon, levels, per_node, chunks, narrow = dims
    width = 2 * fields
    per_group = LANES // width
    groups = padded // per_group
    chunk = nlon // chunks

    grid_copies = []
    for c in range(chunks):
        part = pl.ds(c * chunk, chunk)
        copy = pltpu.make_async_copy(grid_hbm.at[:, part], grid_ref.at[c], grid_sem.at[c])
        copy.start()
        grid_copies.append(copy)
    leaf_copy = pltpu.make_async_copy(leaf_hbm, leaf_ref, weight_sem.at[0])
    leaf_copy.start()
    transfer_copies = []
    for b in range(levels):
        copy = pltpu.make_async_copy(transfer_hbm.at[b], transfer_ref.at[b], weight_sem.at[2 + b])
        copy.start()
        transfer_copies.append(copy)
    degree_copy = pltpu.make_async_copy(degree_hbm, degree_ref, weight_sem.at[1])
    degree_copy.start()

    me = lax.axis_index("lat")
    uppers, partners = [], []
    barrier = pltpu.get_barrier_semaphore()
    for b in range(levels):
        upper = me // 2**b % 2
        partner = me + (1 - 2 * upper) * 2**b
        uppers.append(upper)
        partners.append(partner)
        pl.semaphore_signal(barrier, inc=1, device_id={"lat": partner}, device_id_type=MESH)

    row = lax.broadcasted_iota(jnp.int32, (padded, LANES), 0)
    lane = lax.broadcasted_iota(jnp.int32, (padded, LANES), 1)
    order = jnp.zeros((padded, LANES), jnp.int32)
    for o in range(orders):
        order = jnp.where(row == o, ids_ref[o], order)
    unit = jnp.float32(2.0 * math.pi / nlon)
    wrap = (lambda v: v & (nlon - 1)) if nlon & (nlon - 1) == 0 else (lambda v: v % nlon)
    fine = wrap(order * lane).astype(jnp.float32) * unit
    fine_cos, fine_sin = jnp.cos(fine), jnp.sin(fine)
    steps = nlon // LANES
    coarse_parts = []
    for first in range(0, steps, LANES):
        coarse = wrap(wrap(order * LANES) * (lane + first)).astype(jnp.float32) * unit
        coarse_parts.append((jnp.cos(coarse), jnp.sin(coarse)))

    for c in range(chunks):
        for a in range(c * chunk // LANES, (c + 1) * chunk // LANES):
            coarse_cos, coarse_sin = coarse_parts[a // LANES]
            at = a % LANES
            cos_a = coarse_cos[:, at : at + 1]
            sin_a = coarse_sin[:, at : at + 1]
            real = cos_a * fine_cos - sin_a * fine_sin
            imaginary = -(sin_a * fine_cos + cos_a * fine_sin)
            both = jnp.concatenate([real, imaginary], axis=0).astype(jnp.bfloat16)
            table_ref[:, a * LANES : (a + 1) * LANES] = both
        grid_copies[c].wait()
        piece = lax.dot_general(
            grid_ref[c],
            table_ref[:, c * chunk : (c + 1) * chunk],
            (((1,), (1,)), ((), ())),
            preferred_element_type=jnp.float32,
        )
        if c == 0:
            raw_ref[:, : 2 * padded] = piece
        else:
            raw_ref[:, : 2 * padded] += piece

    scale = weight_ref[...] / jnp.float32(math.sqrt(nlon))
    for f in range(fields):
        flat = raw_ref[pl.ds(f, cycles, stride=fields), :].T
        waves_ref[pl.ds(f, padded, stride=width), :] = flat[:padded] * scale
        waves_ref[pl.ds(fields + f, padded, stride=width), :] = flat[padded : 2 * padded] * scale

    copies = []

    def send(b, g):
        mine = pl.ds(pl.multiple_of(uppers[b] * rank, rank), rank)
        for i, ref in enumerate((high_ref, low_ref)[: 1 if narrow[b] else 2]):
            copy = pltpu.make_async_remote_copy(
                src_ref=ref.at[b, g, mine],
                dst_ref=ref.at[b, g, mine],
                send_sem=send_sem.at[b, g, i],
                recv_sem=recv_sem.at[b, g, i],
                device_id={"lat": partners[b]},
                device_id_type=MESH,
            )
            copy.start()
            copies.append(copy)
            pending[b, g, i] = copy

    def keep(b, g, value):
        mine = pl.ds(pl.multiple_of(uppers[b] * rank, rank), rank)
        high, low = split(value)
        high_ref[b, g, mine] = high
        low_ref[b, g, mine] = low

    pending = {}
    for b in range(levels):
        if narrow[b]:
            theirs = pl.ds(pl.multiple_of((1 - uppers[b]) * rank, rank), rank)
            for g in range(groups):
                low_ref[b, g, theirs] = jnp.zeros((rank, LANES), jnp.bfloat16)

    leaf_copy.wait()
    slot = lax.broadcasted_iota(jnp.int32, (rank, LANES), 1) // width

    def members(g):
        return min(per_group, orders - g * per_group)

    for g in range(groups):
        rows = []
        for p in range(per_group):
            o = g * per_group + p
            if o < orders:
                high, low = split(waves_ref[o * width : (o + 1) * width, :])
                both = jnp.dot(
                    jnp.concatenate([high, low], axis=0),
                    leaf_ref[o * cycles : (o + 1) * cycles, :],
                    preferred_element_type=jnp.float32,
                )
                rows.append(both[:width] + both[width:])
            else:
                rows.append(jnp.zeros((width, rank), jnp.float32))
        keep(0, g, jnp.concatenate(rows, axis=0).T)
        if g == 0:
            pl.semaphore_wait(barrier, levels)
        send(0, g)

    degree_base = me * per_node
    degree_id = degree_base + lax.broadcasted_iota(jnp.int32, (width, per_node), 1)
    for b in range(levels):
        transfer_copies[b].wait()
        if b == levels - 1:
            degree_copy.wait()
        for g in range(groups):
            count = members(g)
            for i in range(1 if narrow[b] else 2):
                pending[b, g, i].wait_recv()
            first = g * per_group * rank
            both = jnp.dot(
                transfer_ref[b, first : first + count * rank, :],
                jnp.concatenate([high_ref[b, g], low_ref[b, g]], axis=1),
                preferred_element_type=jnp.float32,
            )
            value = jnp.zeros((rank, LANES), jnp.float32)
            for p in range(count):
                block = both[p * rank : (p + 1) * rank]
                value = jnp.where(slot == p, block[:, :LANES] + block[:, LANES:], value)
            if b < levels - 1:
                keep(b + 1, g, value)
                send(b + 1, g)
            else:
                high, low = split(value.T)
                for p in range(count):
                    o = g * per_group + p
                    mine = slice(p * width, (p + 1) * width)
                    final = jnp.dot(
                        jnp.concatenate([high[mine], low[mine]], axis=0),
                        degree_ref[o * rank : (o + 1) * rank, :],
                        preferred_element_type=jnp.float32,
                    )
                    final = final[:width] + final[width:]
                    out_ref[o] = jnp.where(degree_id >= ids_ref[o], final, 0.0)

    for copy in copies:
        copy.wait_send()


def body(grid, cycle_weights, order_ids, leaf_weight, transfer, degree_weight):
    cycles, fields, nlon = grid.shape
    orders = order_ids.shape[0]
    rank = leaf_weight.shape[2]
    levels = transfer.shape[0]
    per_node = degree_weight.shape[0]
    width = 2 * fields
    per_group = LANES // width
    padded = -(-orders // per_group) * per_group
    groups = padded // per_group
    chunks = 8 if nlon % (8 * LANES) == 0 else 1
    narrow = tuple(b >= max(1, levels - NARROW_LEVELS) for b in range(levels))
    dims = (orders, padded, rank, fields, cycles, nlon, levels, per_node, chunks, narrow)
    hbm = pl.BlockSpec(memory_space=pltpu.HBM)
    vmem = pl.BlockSpec(memory_space=pltpu.VMEM)
    smem = pl.BlockSpec(memory_space=pltpu.SMEM)
    result = pl.pallas_call(
        functools.partial(kernel, dims),
        out_shape=jax.ShapeDtypeStruct((orders, width, per_node), jnp.float32),
        in_specs=[smem, vmem, hbm, hbm, hbm, hbm],
        out_specs=vmem,
        scratch_shapes=[
            pltpu.VMEM((chunks, cycles * fields, nlon // chunks), jnp.bfloat16),
            pltpu.VMEM((orders * cycles, rank), jnp.bfloat16),
            pltpu.VMEM((levels, orders * rank, 2 * rank), jnp.bfloat16),
            pltpu.VMEM((orders * rank, per_node), jnp.bfloat16),
            pltpu.VMEM((2 * padded, nlon), jnp.bfloat16),
            pltpu.VMEM((cycles * fields, LANES), jnp.float32),
            pltpu.VMEM((padded * width, cycles), jnp.float32),
            pltpu.VMEM((levels, groups, 2 * rank, LANES), jnp.bfloat16),
            pltpu.VMEM((levels, groups, 2 * rank, LANES), jnp.bfloat16),
            pltpu.SemaphoreType.DMA((chunks,)),
            pltpu.SemaphoreType.DMA((2 + levels,)),
            pltpu.SemaphoreType.DMA((levels, groups, 2)),
            pltpu.SemaphoreType.DMA((levels, groups, 2)),
        ],
        compiler_params=pltpu.CompilerParams(
            collective_id=0, has_side_effects=True, vmem_limit_bytes=56 * 2**20
        ),
        name="analysis",
    )(
        order_ids,
        cycle_weights.reshape(1, cycles),
        grid.reshape(cycles * fields, nlon),
        leaf_weight.transpose(1, 0, 2).reshape(orders * cycles, rank),
        transfer.reshape(levels, orders * rank, 2 * rank),
        degree_weight.transpose(1, 2, 0).reshape(orders * rank, per_node),
    )
    return result.transpose(2, 0, 1)


def solution(mesh):
    return jax.shard_map(
        body,
        mesh=mesh,
        in_specs=(
            P("lat", "groups", None),
            P("lat"),
            P(),
            P("lat", None, None),
            P(None, "lat", None, None, None),
            P("lat", None, None),
        ),
        out_specs=P("lat", None, "groups"),
        check_vma=False,
    )
```

```python
import functools
import math

import jax
import jax.numpy as jnp
from jax import lax
from jax.experimental import pallas as pl
from jax.experimental.pallas import tpu as pltpu
from jax.sharding import PartitionSpec as P

LANES = 128
NARROW_LEVELS = 3
MESH = pl.DeviceIdType.MESH


def split(x):
    high = x.astype(jnp.bfloat16)
    low = (x - high.astype(jnp.float32)).astype(jnp.bfloat16)
    return high, low


def cos_sin(turn, count):
    x = (turn.astype(jnp.float32) - jnp.float32(count / 2)) * jnp.float32(2.0 * math.pi / count)
    square = x * x
    even = jnp.full_like(x, 1.0 / math.factorial(16))
    odd = jnp.full_like(x, 1.0 / math.factorial(17))
    for n in range(14, -1, -2):
        sign = -1.0 if n // 2 % 2 else 1.0
        even = even * square + jnp.float32(sign / math.factorial(n))
        odd = odd * square + jnp.float32(sign / math.factorial(n + 1))
    return -even, -(odd * x)


def kernel(
    dims,
    ids_ref,
    weight_ref,
    grid_hbm,
    leaf_hbm,
    transfer_hbm,
    degree_hbm,
    out_ref,
    grid_ref,
    leaf_ref,
    transfer_ref,
    degree_ref,
    table_ref,
    raw_ref,
    waves_ref,
    high_ref,
    low_ref,
    grid_sem,
    weight_sem,
    send_sem,
    recv_sem,
):
    orders, padded, rank, fields, cycles, nlon, levels, per_node, chunks, narrow = dims
    width = 2 * fields
    per_group = LANES // width
    groups = padded // per_group
    chunk = nlon // chunks

    grid_copies = []
    for c in range(chunks):
        part = pl.ds(c * chunk, chunk)
        copy = pltpu.make_async_copy(grid_hbm.at[:, part], grid_ref.at[c], grid_sem.at[c])
        copy.start()
        grid_copies.append(copy)
    leaf_copy = pltpu.make_async_copy(leaf_hbm, leaf_ref, weight_sem.at[0])
    leaf_copy.start()
    transfer_copies = []
    for b in range(levels):
        copy = pltpu.make_async_copy(transfer_hbm.at[b], transfer_ref.at[b], weight_sem.at[2 + b])
        transfer_copies.append(copy)
    degree_copy = pltpu.make_async_copy(degree_hbm, degree_ref, weight_sem.at[1])

    me = lax.axis_index("lat")
    uppers, partners = [], []
    barrier = pltpu.get_barrier_semaphore()
    for b in range(levels):
        upper = me // 2**b % 2
        partner = me + (1 - 2 * upper) * 2**b
        uppers.append(upper)
        partners.append(partner)
        pl.semaphore_signal(barrier, inc=1, device_id={"lat": partner}, device_id_type=MESH)

    row = lax.broadcasted_iota(jnp.int32, (padded, LANES), 0)
    lane = lax.broadcasted_iota(jnp.int32, (padded, LANES), 1)
    order = jnp.zeros((padded, LANES), jnp.int32)
    for o in range(orders):
        order = jnp.where(row == o, ids_ref[o], order)
    wrap = (lambda v: v & (nlon - 1)) if nlon & (nlon - 1) == 0 else (lambda v: v % nlon)
    fine_cos, fine_sin = cos_sin(wrap(order * lane), nlon)
    steps = nlon // LANES
    coarse_parts = []
    for first in range(0, steps, LANES):
        coarse_parts.append(cos_sin(wrap(wrap(order * LANES) * (lane + first)), nlon))

    for c in range(chunks):
        for a in range(c * chunk // LANES, (c + 1) * chunk // LANES):
            coarse_cos, coarse_sin = coarse_parts[a // LANES]
            at = a % LANES
            cos_a = coarse_cos[:, at : at + 1]
            sin_a = coarse_sin[:, at : at + 1]
            real = cos_a * fine_cos - sin_a * fine_sin
            imaginary = -(sin_a * fine_cos + cos_a * fine_sin)
            both = jnp.concatenate([real, imaginary], axis=0).astype(jnp.bfloat16)
            table_ref[:, a * LANES : (a + 1) * LANES] = both
        grid_copies[c].wait()
        if c == chunks - 1:
            for copy in transfer_copies + [degree_copy]:
                copy.start()
        piece = lax.dot_general(
            table_ref[:, c * chunk : (c + 1) * chunk],
            grid_ref[c],
            (((1,), (1,)), ((), ())),
            preferred_element_type=jnp.float32,
        )
        total = piece if c == 0 else total + piece
    raw_ref[:, : 2 * padded] = total.T

    scale = weight_ref[...] / jnp.float32(math.sqrt(nlon))
    for f in range(fields):
        flat = raw_ref[pl.ds(f, cycles, stride=fields), :].T
        waves_ref[pl.ds(f, padded, stride=width), :] = flat[:padded] * scale
        waves_ref[pl.ds(fields + f, padded, stride=width), :] = flat[padded : 2 * padded] * scale

    copies = []

    def send(b, g):
        mine = pl.ds(pl.multiple_of(uppers[b] * rank, rank), rank)
        for i, ref in enumerate((high_ref, low_ref)[: 1 if narrow[b] else 2]):
            copy = pltpu.make_async_remote_copy(
                src_ref=ref.at[b, g, mine],
                dst_ref=ref.at[b, g, mine],
                send_sem=send_sem.at[b, g, i],
                recv_sem=recv_sem.at[b, g, i],
                device_id={"lat": partners[b]},
                device_id_type=MESH,
            )
            copy.start()
            copies.append(copy)
            pending[b, g, i] = copy

    def keep(b, g, value):
        mine = pl.ds(pl.multiple_of(uppers[b] * rank, rank), rank)
        high, low = split(value)
        high_ref[b, g, mine] = high
        low_ref[b, g, mine] = low

    pending = {}
    for b in range(levels):
        if narrow[b]:
            theirs = pl.ds(pl.multiple_of((1 - uppers[b]) * rank, rank), rank)
            for g in range(groups):
                low_ref[b, g, theirs] = jnp.zeros((rank, LANES), jnp.bfloat16)

    leaf_copy.wait()
    slot = lax.broadcasted_iota(jnp.int32, (rank, LANES), 1) // width

    def members(g):
        return min(per_group, orders - g * per_group)

    for g in range(groups):
        rows = []
        for p in range(per_group):
            o = g * per_group + p
            if o < orders:
                high, low = split(waves_ref[o * width : (o + 1) * width, :])
                both = jnp.dot(
                    jnp.concatenate([high, low], axis=0),
                    leaf_ref[o * cycles : (o + 1) * cycles, :],
                    preferred_element_type=jnp.float32,
                )
                rows.append(both[:width] + both[width:])
            else:
                rows.append(jnp.zeros((width, rank), jnp.float32))
        keep(0, g, jnp.concatenate(rows, axis=0).T)
        if g == 0:
            pl.semaphore_wait(barrier, levels)
        send(0, g)

    degree_base = me * per_node
    degree_id = degree_base + lax.broadcasted_iota(jnp.int32, (width, per_node), 1)
    for b in range(levels):
        transfer_copies[b].wait()
        if b == levels - 1:
            degree_copy.wait()
        for g in range(groups):
            count = members(g)
            for i in range(1 if narrow[b] else 2):
                pending[b, g, i].wait_recv()
            first = g * per_group * rank
            both = jnp.dot(
                transfer_ref[b, first : first + count * rank, :],
                jnp.concatenate([high_ref[b, g], low_ref[b, g]], axis=1),
                preferred_element_type=jnp.float32,
            )
            value = jnp.zeros((rank, LANES), jnp.float32)
            for p in range(count):
                block = both[p * rank : (p + 1) * rank]
                value = jnp.where(slot == p, block[:, :LANES] + block[:, LANES:], value)
            if b < levels - 1:
                keep(b + 1, g, value)
                send(b + 1, g)
            else:
                high, low = split(value.T)
                for p in range(count):
                    o = g * per_group + p
                    mine = slice(p * width, (p + 1) * width)
                    final = jnp.dot(
                        jnp.concatenate([high[mine], low[mine]], axis=0),
                        degree_ref[o * rank : (o + 1) * rank, :],
                        preferred_element_type=jnp.float32,
                    )
                    final = final[:width] + final[width:]
                    out_ref[o] = jnp.where(degree_id >= ids_ref[o], final, 0.0)

    for copy in copies:
        copy.wait_send()


def body(grid, cycle_weights, order_ids, leaf_weight, transfer, degree_weight):
    cycles, fields, nlon = grid.shape
    orders = order_ids.shape[0]
    rank = leaf_weight.shape[2]
    levels = transfer.shape[0]
    per_node = degree_weight.shape[0]
    width = 2 * fields
    per_group = LANES // width
    padded = -(-orders // per_group) * per_group
    groups = padded // per_group
    chunks = 16 if nlon % (16 * LANES) == 0 else 1
    narrow = tuple(b >= max(1, levels - NARROW_LEVELS) for b in range(levels))
    dims = (orders, padded, rank, fields, cycles, nlon, levels, per_node, chunks, narrow)
    hbm = pl.BlockSpec(memory_space=pltpu.HBM)
    vmem = pl.BlockSpec(memory_space=pltpu.VMEM)
    smem = pl.BlockSpec(memory_space=pltpu.SMEM)
    result = pl.pallas_call(
        functools.partial(kernel, dims),
        out_shape=jax.ShapeDtypeStruct((orders, width, per_node), jnp.float32),
        in_specs=[smem, vmem, hbm, hbm, hbm, hbm],
        out_specs=vmem,
        scratch_shapes=[
            pltpu.VMEM((chunks, cycles * fields, nlon // chunks), jnp.bfloat16),
            pltpu.VMEM((orders * cycles, rank), jnp.bfloat16),
            pltpu.VMEM((levels, orders * rank, 2 * rank), jnp.bfloat16),
            pltpu.VMEM((orders * rank, per_node), jnp.bfloat16),
            pltpu.VMEM((2 * padded, nlon), jnp.bfloat16),
            pltpu.VMEM((cycles * fields, LANES), jnp.float32),
            pltpu.VMEM((padded * width, cycles), jnp.float32),
            pltpu.VMEM((levels, groups, 2 * rank, LANES), jnp.bfloat16),
            pltpu.VMEM((levels, groups, 2 * rank, LANES), jnp.bfloat16),
            pltpu.SemaphoreType.DMA((chunks,)),
            pltpu.SemaphoreType.DMA((2 + levels,)),
            pltpu.SemaphoreType.DMA((levels, groups, 2)),
            pltpu.SemaphoreType.DMA((levels, groups, 2)),
        ],
        compiler_params=pltpu.CompilerParams(
            collective_id=0, has_side_effects=True, vmem_limit_bytes=56 * 2**20
        ),
        name="analysis",
    )(
        order_ids,
        cycle_weights.reshape(1, cycles),
        grid.reshape(cycles * fields, nlon),
        leaf_weight.transpose(1, 0, 2).reshape(orders * cycles, rank),
        transfer.reshape(levels, orders * rank, 2 * rank),
        degree_weight.transpose(1, 2, 0).reshape(orders * rank, per_node),
    )
    return result.transpose(2, 0, 1)


def solution(mesh):
    return jax.shard_map(
        body,
        mesh=mesh,
        in_specs=(
            P("lat", "groups", None),
            P("lat"),
            P(),
            P("lat", None, None),
            P(None, "lat", None, None, None),
            P("lat", None, None),
        ),
        out_specs=P("lat", None, "groups"),
        check_vma=False,
    )
```

```python
import functools
import math

import jax
import jax.numpy as jnp
from jax import lax
from jax.experimental import pallas as pl
from jax.experimental.pallas import tpu as pltpu
from jax.sharding import PartitionSpec as P

LANES = 128
NARROW_LEVELS = 3
MESH = pl.DeviceIdType.MESH


def split(x):
    high = x.astype(jnp.bfloat16)
    low = (x - high.astype(jnp.float32)).astype(jnp.bfloat16)
    return high, low


def cos_sin(turn, count):
    x = (turn.astype(jnp.float32) - jnp.float32(count / 2)) * jnp.float32(2.0 * math.pi / count)
    square = x * x
    even = jnp.full_like(x, 1.0 / math.factorial(16))
    odd = jnp.full_like(x, 1.0 / math.factorial(17))
    for n in range(14, -1, -2):
        sign = -1.0 if n // 2 % 2 else 1.0
        even = even * square + jnp.float32(sign / math.factorial(n))
        odd = odd * square + jnp.float32(sign / math.factorial(n + 1))
    return -even, -(odd * x)


def kernel(
    dims,
    ids_ref,
    weight_ref,
    grid_hbm,
    leaf_hbm,
    transfer_hbm,
    degree_hbm,
    out_hbm,
    out_ref,
    grid_ref,
    leaf_ref,
    transfer_ref,
    degree_ref,
    table_ref,
    raw_ref,
    waves_ref,
    high_ref,
    low_ref,
    grid_sem,
    weight_sem,
    send_sem,
    recv_sem,
    out_sem,
):
    orders, padded, rank, fields, cycles, nlon, levels, per_node, chunks, narrow = dims
    width = 2 * fields
    per_group = LANES // width
    groups = padded // per_group
    chunk = nlon // chunks

    grid_copies = []
    for c in range(chunks):
        part = pl.ds(c * chunk, chunk)
        copy = pltpu.make_async_copy(grid_hbm.at[:, part], grid_ref.at[c], grid_sem.at[c])
        copy.start()
        grid_copies.append(copy)
    leaf_copy = pltpu.make_async_copy(leaf_hbm, leaf_ref, weight_sem.at[0])
    leaf_copy.start()
    transfer_copies = []
    for b in range(levels):
        copy = pltpu.make_async_copy(transfer_hbm.at[b], transfer_ref.at[b], weight_sem.at[2 + b])
        transfer_copies.append(copy)
    degree_copy = pltpu.make_async_copy(degree_hbm, degree_ref, weight_sem.at[1])

    me = lax.axis_index("lat")
    uppers, partners = [], []
    barrier = pltpu.get_barrier_semaphore()
    for b in range(levels):
        upper = me // 2**b % 2
        partner = me + (1 - 2 * upper) * 2**b
        uppers.append(upper)
        partners.append(partner)
        pl.semaphore_signal(barrier, inc=1, device_id={"lat": partner}, device_id_type=MESH)

    row = lax.broadcasted_iota(jnp.int32, (padded, LANES), 0)
    lane = lax.broadcasted_iota(jnp.int32, (padded, LANES), 1)
    order = jnp.zeros((padded, LANES), jnp.int32)
    for o in range(orders):
        order = jnp.where(row == o, ids_ref[o], order)
    wrap = (lambda v: v & (nlon - 1)) if nlon & (nlon - 1) == 0 else (lambda v: v % nlon)
    fine_cos, fine_sin = cos_sin(wrap(order * lane), nlon)
    steps = nlon // LANES
    coarse_parts = []
    for first in range(0, steps, LANES):
        coarse_parts.append(cos_sin(wrap(wrap(order * LANES) * (lane + first)), nlon))

    for c in range(chunks):
        for a in range(c * chunk // LANES, (c + 1) * chunk // LANES):
            coarse_cos, coarse_sin = coarse_parts[a // LANES]
            at = a % LANES
            cos_a = coarse_cos[:, at : at + 1]
            sin_a = coarse_sin[:, at : at + 1]
            real = cos_a * fine_cos - sin_a * fine_sin
            imaginary = -(sin_a * fine_cos + cos_a * fine_sin)
            both = jnp.concatenate([real, imaginary], axis=0).astype(jnp.bfloat16)
            table_ref[:, a * LANES : (a + 1) * LANES] = both
        grid_copies[c].wait()
        if c == chunks - 1:
            for copy in transfer_copies + [degree_copy]:
                copy.start()
        piece = lax.dot_general(
            table_ref[:, c * chunk : (c + 1) * chunk],
            grid_ref[c],
            (((1,), (1,)), ((), ())),
            preferred_element_type=jnp.float32,
        )
        total = piece if c == 0 else total + piece
    raw_ref[:, : 2 * padded] = total.T

    scale = weight_ref[...] / jnp.float32(math.sqrt(nlon))
    for f in range(fields):
        flat = raw_ref[pl.ds(f, cycles, stride=fields), :].T
        waves_ref[pl.ds(f, padded, stride=width), :] = flat[:padded] * scale
        waves_ref[pl.ds(fields + f, padded, stride=width), :] = flat[padded : 2 * padded] * scale

    copies, out_copies = [], []

    def send(b, g):
        mine = pl.ds(pl.multiple_of(uppers[b] * rank, rank), rank)
        for i, ref in enumerate((high_ref, low_ref)[: 1 if narrow[b] else 2]):
            copy = pltpu.make_async_remote_copy(
                src_ref=ref.at[b, g, mine],
                dst_ref=ref.at[b, g, mine],
                send_sem=send_sem.at[b, g, i],
                recv_sem=recv_sem.at[b, g, i],
                device_id={"lat": partners[b]},
                device_id_type=MESH,
            )
            copy.start()
            copies.append(copy)
            pending[b, g, i] = copy

    def keep(b, g, value):
        mine = pl.ds(pl.multiple_of(uppers[b] * rank, rank), rank)
        high, low = split(value)
        high_ref[b, g, mine] = high
        low_ref[b, g, mine] = low

    pending = {}
    for b in range(levels):
        if narrow[b]:
            theirs = pl.ds(pl.multiple_of((1 - uppers[b]) * rank, rank), rank)
            for g in range(groups):
                low_ref[b, g, theirs] = jnp.zeros((rank, LANES), jnp.bfloat16)

    leaf_copy.wait()
    slot = lax.broadcasted_iota(jnp.int32, (rank, LANES), 1) // width

    def members(g):
        return min(per_group, orders - g * per_group)

    for g in range(groups):
        rows = []
        for p in range(per_group):
            o = g * per_group + p
            if o < orders:
                high, low = split(waves_ref[o * width : (o + 1) * width, :])
                both = jnp.dot(
                    jnp.concatenate([high, low], axis=0),
                    leaf_ref[o * cycles : (o + 1) * cycles, :],
                    preferred_element_type=jnp.float32,
                )
                rows.append(both[:width] + both[width:])
            else:
                rows.append(jnp.zeros((width, rank), jnp.float32))
        keep(0, g, jnp.concatenate(rows, axis=0).T)
        if g == 0:
            pl.semaphore_wait(barrier, levels)
        send(0, g)

    degree_base = me * per_node
    degree_id = degree_base + lax.broadcasted_iota(jnp.int32, (width, per_node), 1)
    for b in range(levels):
        transfer_copies[b].wait()
        if b == levels - 1:
            degree_copy.wait()
        for g in range(groups):
            count = members(g)
            for i in range(1 if narrow[b] else 2):
                pending[b, g, i].wait_recv()
            first = g * per_group * rank
            both = jnp.dot(
                transfer_ref[b, first : first + count * rank, :],
                jnp.concatenate([high_ref[b, g], low_ref[b, g]], axis=1),
                preferred_element_type=jnp.float32,
            )
            value = jnp.zeros((rank, LANES), jnp.float32)
            for p in range(count):
                block = both[p * rank : (p + 1) * rank]
                value = jnp.where(slot == p, block[:, :LANES] + block[:, LANES:], value)
            if b < levels - 1:
                keep(b + 1, g, value)
                send(b + 1, g)
            else:
                high, low = split(value.T)
                for p in range(count):
                    o = g * per_group + p
                    mine = slice(p * width, (p + 1) * width)
                    final = jnp.dot(
                        jnp.concatenate([high[mine], low[mine]], axis=0),
                        degree_ref[o * rank : (o + 1) * rank, :],
                        preferred_element_type=jnp.float32,
                    )
                    final = final[:width] + final[width:]
                    out_ref[o] = jnp.where(degree_id >= ids_ref[o], final, 0.0)
                done = pl.ds(g * per_group, count)
                copy = pltpu.make_async_copy(out_ref.at[done], out_hbm.at[done], out_sem.at[g])
                copy.start()
                out_copies.append(copy)

    for copy in copies:
        copy.wait_send()
    for copy in out_copies:
        copy.wait()


def body(grid, cycle_weights, order_ids, leaf_weight, transfer, degree_weight):
    cycles, fields, nlon = grid.shape
    orders = order_ids.shape[0]
    rank = leaf_weight.shape[2]
    levels = transfer.shape[0]
    per_node = degree_weight.shape[0]
    width = 2 * fields
    per_group = LANES // width
    padded = -(-orders // per_group) * per_group
    groups = padded // per_group
    chunks = 16 if nlon % (16 * LANES) == 0 else 1
    narrow = tuple(b >= max(1, levels - NARROW_LEVELS) for b in range(levels))
    dims = (orders, padded, rank, fields, cycles, nlon, levels, per_node, chunks, narrow)
    hbm = pl.BlockSpec(memory_space=pltpu.HBM)
    vmem = pl.BlockSpec(memory_space=pltpu.VMEM)
    smem = pl.BlockSpec(memory_space=pltpu.SMEM)
    result = pl.pallas_call(
        functools.partial(kernel, dims),
        out_shape=jax.ShapeDtypeStruct((orders, width, per_node), jnp.float32),
        in_specs=[smem, vmem, hbm, hbm, hbm, hbm],
        out_specs=hbm,
        scratch_shapes=[
            pltpu.VMEM((orders, width, per_node), jnp.float32),
            pltpu.VMEM((chunks, cycles * fields, nlon // chunks), jnp.bfloat16),
            pltpu.VMEM((orders * cycles, rank), jnp.bfloat16),
            pltpu.VMEM((levels, orders * rank, 2 * rank), jnp.bfloat16),
            pltpu.VMEM((orders * rank, per_node), jnp.bfloat16),
            pltpu.VMEM((2 * padded, nlon), jnp.bfloat16),
            pltpu.VMEM((cycles * fields, LANES), jnp.float32),
            pltpu.VMEM((padded * width, cycles), jnp.float32),
            pltpu.VMEM((levels, groups, 2 * rank, LANES), jnp.bfloat16),
            pltpu.VMEM((levels, groups, 2 * rank, LANES), jnp.bfloat16),
            pltpu.SemaphoreType.DMA((chunks,)),
            pltpu.SemaphoreType.DMA((2 + levels,)),
            pltpu.SemaphoreType.DMA((levels, groups, 2)),
            pltpu.SemaphoreType.DMA((levels, groups, 2)),
            pltpu.SemaphoreType.DMA((groups,)),
        ],
        compiler_params=pltpu.CompilerParams(
            collective_id=0, has_side_effects=True, vmem_limit_bytes=56 * 2**20
        ),
        name="analysis",
    )(
        order_ids,
        cycle_weights.reshape(1, cycles),
        grid.reshape(cycles * fields, nlon),
        leaf_weight.transpose(1, 0, 2).reshape(orders * cycles, rank),
        transfer.reshape(levels, orders * rank, 2 * rank),
        degree_weight.transpose(1, 2, 0).reshape(orders * rank, per_node),
    )
    return result.transpose(2, 0, 1)


def solution(mesh):
    return jax.shard_map(
        body,
        mesh=mesh,
        in_specs=(
            P("lat", "groups", None),
            P("lat"),
            P(),
            P("lat", None, None),
            P(None, "lat", None, None, None),
            P("lat", None, None),
        ),
        out_specs=P("lat", None, "groups"),
        check_vma=False,
    )
```
